32 devices in a mesh: rep: 2 (over x), ep: 16 (over z, y, core).
Axes of the slice: x: 2, y: 2, z: 4, core: 2. Of those that a mesh axis runs over, the one named last changes fastest.
Arguments:
- hidden_in: bfloat16 [4, 64, 7168], P(None, 'ep'), may hold values from -6 to 6
- queries: bfloat16 [4, 64, 8192], P(None, None, 'ep'), may hold values from -216 to 216
- new_keys: bfloat16 [4, 64, 8192], P(None, None, 'ep'), may hold values from -6 to 6
- new_values: bfloat16 [4, 64, 8192], P(None, None, 'ep'), may hold values from -6 to 6
- cache_keys: bfloat16 [64, 32, 8192], P(None, None, 'ep'), may hold values from -6 to 6
- cache_values: bfloat16 [64, 32, 8192], P(None, None, 'ep'), may hold values from -6 to 6
- cache_lengths: int32 [64], replicated, may hold values from 1 to 32, 1056 in all
- expert_ids: int32 [4, 64, 8], P(None, 'ep'), may hold values from 0 to 15, all different within a row; in each aligned block of 4 rows (0 to 3, 4 to 7, ..., all dimensions but the last counted through in order) at most 4 rows name the same one
- router_logits: float32 [4, 64, 8], P(None, 'ep'), may hold values from -6 to 6
- norm_gain: float32 [7168], replicated, may hold values from 0.1 to 1.9
- out_sectioned: bfloat16 [8192, 7168], P('ep', 'rep'), may hold values from -0.0625 to 0.0625
- expert_sectioned: bfloat16 [16, 7168, 3, 1024], P('ep', 'rep'), may hold values from -0.09375 to 0.09375
- bucket_owner: int32 [16, 2], P('ep'), may hold values from 0 to 1, each once within a row
Outputs:
- layer_out: bfloat16 [4, 64, 7168], P(None, 'ep')
The draws below stay inside these ranges and needn't reach their ends.
Inputs may be any that keep to these rules, and one draw needn't show every extreme that they name: `expert_ids`: within one step, the rows of one device (aligned blocks of 4 rows) name no expert more than 4 times; some expert is named exactly 4 times. Each row names distinct experts. `bucket_owner`: for each expert the owners of its 2 buckets are distinct.
All inputs are finite; a program needn't handle non-finite values.
Results may differ from the reference program's by a relative error of at most 0.025.
Values may be sent and summed in bfloat16 or wider, within the bound.
A program may use at most 192 MiB of HBM per device.

```python
import math
import jax
import jax.numpy as jnp
import numpy as np
from jax import lax

D = 7168
H = 64
DH = 128
FFE = 1024
TOPK = 8
STEPS = 4
ROWS = 64
CACHE = 32
EXPERTS = 16
CAP = 4
N_REP = 2
N_EP = 16


def shared_keys(key):
    return jnp.clip(jax.random.normal(key, (ROWS, CACHE, H * DH), jnp.float32), -6.0, 6.0)


def draw_cache_keys(key, part):
    base = shared_keys(key)
    return base.astype(jnp.bfloat16)


def draw_queries(key, part):
    key = jax.random.fold_in(key, 7)
    fresh = jnp.clip(jax.random.normal(key, (STEPS, ROWS, H * DH), jnp.float32), -6.0, 6.0)
    return fresh.astype(jnp.bfloat16)


def level_of(rng, shape, cuts, low, high):
    loudness = 1.0
    for position, parts in cuts:
        steps = jax.random.uniform(jax.random.fold_in(jax.random.fold_in(rng, 6), position), (parts,), jnp.float32, low / len(cuts), high / len(cuts))
        loudness = loudness * jnp.repeat(jnp.exp(steps), shape[position] // parts).reshape((-1,) + (1,) * (len(shape) - 1 - position))
    return loudness


def split_up(count, total, bound, slope):
    loads = [(1 << 20) // math.isqrt(grade ** slope) + 1 for grade in range(2, count + 1)]
    spare, counts = total - bound - (count - 1), [1] * (count - 1)
    while spare > 0:
        candidates = [i for i in range(count - 1) if counts[i] < bound]
        whole, budget = sum([loads[i] for i in candidates]), spare
        for i in candidates:
            more = min(bound - counts[i], max(1, budget * loads[i] // whole), spare)
            counts[i] = counts[i] + more
            spare = spare - more
    return np.array([bound] + counts)


def ragged(rng, amount, total, limit, slope):
    if amount == 2:
        one = jax.random.randint(rng, (), max(1, total - limit), min(limit, total - 1) + 1)
        return jnp.stack([one, total - one])
    lengths = jnp.asarray(split_up(amount, total, limit, slope), jnp.int32)
    twos = (amount - 1) // 2
    source_of, sink = lengths[1:1 + 2 * twos:2], lengths[2:2 + 2 * twos:2]
    slack = jnp.minimum(source_of - 1, limit - sink)
    passed = jax.random.randint(jax.random.fold_in(rng, 1), (twos,), 0, 1 << 20) % (slack + 1)
    lengths = lengths.at[1:1 + 2 * twos:2].set(source_of - passed).at[2:2 + 2 * twos:2].set(sink + passed)
    return lengths[jax.random.permutation(jax.random.fold_in(rng, 2), amount)]


def assign_block(rng, own, number, rows, amount, top, reach, skew):
    sequence = jax.random.permutation(rng, amount)
    heavy_load, common = portions_of(amount, rows * top, reach, skew, True), portions_of(amount, rows * top, reach, skew, False)
    places = jnp.arange(amount)

    def named(lengths, turn):
        used = int((lengths > 0).sum())
        fixed = max(1, used // 4)
        moved = fixed + (places - fixed + turn * (used - fixed)) % max(1, amount - fixed)
        return jnp.zeros((amount,), jnp.int32).at[sequence[jnp.where(places < fixed, places, moved)]].set(jnp.asarray(lengths, jnp.int32))

    lengths = jnp.where(number % 4 == 0, named(heavy_load, number // 4), named(common, number - number // 4 - 1))
    mixed = jax.random.permutation(jax.random.fold_in(own, 3), amount)
    source_of, receiver = mixed[0:amount // 2 * 2:2], mixed[1:amount // 2 * 2:2]
    margin = jnp.minimum(lengths[source_of] - 1, reach - lengths[receiver]) // 2
    margin = jnp.where((source_of == sequence[0]) | (receiver == sequence[0]) | (lengths[receiver] == 0), 0, jnp.maximum(margin, 0))
    moved = jax.random.randint(jax.random.fold_in(own, 4), (amount // 2,), 0, 1 << 20) % (margin + 1)
    lengths = lengths.at[source_of].add(-moved).at[receiver].add(moved)
    items = jnp.searchsorted(jnp.cumsum(lengths), jnp.arange(rows * top), side="right").astype(jnp.int32)
    grid = items.reshape(top, rows).T
    grid = grid[jax.random.permutation(jax.random.fold_in(own, 1), rows)]
    turn = jax.random.randint(jax.random.fold_in(own, 2), (rows, 1), 0, top)
    return jnp.take_along_axis(grid, (jnp.arange(top)[None, :] + turn) % top, axis=1)


def portions_of(count, total, bound, skew, full):
    loads = [(1 << 20) // math.isqrt(rank ** skew) + 1 for rank in range(1, count + 1)]
    largest = bound if full else min(bound, max(-(-total // count), total * loads[0] // sum(loads)))
    least = 1 if total - largest >= count - 1 else 0
    counts, spare = [largest] + [least] * (count - 1), total - largest - least * (count - 1)
    while spare > 0:
        movable = [i for i in range(1, count) if counts[i] < largest] or [i for i in range(1, count) if counts[i] < bound]
        pool, remaining = sum([loads[i] for i in movable]), spare
        for i in movable:
            addition = min(bound - counts[i], max(1, remaining * loads[i] // pool), spare)
            counts[i] = counts[i] + addition
            spare = spare - addition
    return np.array(counts)


def gaussian(key, shape, deviation, most, cuts=(), kind=jnp.bfloat16):
    gain = level_of(key, shape, cuts, -0.22, 0.18) if cuts else 1.0
    values = jax.random.normal(key, shape, jnp.float32) * deviation * gain
    return jnp.minimum(jnp.maximum(values, -most), most).astype(kind)


def setup_inputs(seed: int = 0) -> dict:
    splits = jax.random.split(jax.random.key(seed), 14)
    hidden_in = gaussian(splits[0], (STEPS, ROWS, D), 1.0, 6.0, ((1, 16),))
    queries = draw_queries(jax.random.fold_in(splits[13], 71), 0)
    new_keys = gaussian(splits[2], (STEPS, ROWS, H * DH), 1.0, 6.0, ((2, 16),))
    new_values = gaussian(splits[3], (STEPS, ROWS, H * DH), 1.0, 6.0, ((2, 16),))
    cache_keys = draw_cache_keys(jax.random.fold_in(splits[13], 71), 0)
    cache_values = gaussian(splits[5], (ROWS, CACHE, H * DH), 1.0, 6.0, ((2, 16),))
    cache_lengths = ragged(splits[6], ROWS, ROWS * (CACHE + 1) // 2, CACHE, 1).astype(jnp.int32)
    expert_ids_keys = jax.random.split(jax.random.fold_in(splits[7], 1), STEPS * ROWS // (ROWS // N_EP))
    expert_ids_turns = jax.random.permutation(jax.random.fold_in(splits[7], 3), STEPS * ROWS // (ROWS // N_EP))
    expert_ids = jax.vmap(lambda own, number: assign_block(jax.random.fold_in(splits[7], 2), own, number, ROWS // N_EP, EXPERTS, TOPK, CAP, 2))(expert_ids_keys, expert_ids_turns).reshape((STEPS, ROWS, TOPK))
    router_logits = gaussian(splits[8], (STEPS, ROWS, TOPK), 1.5, 6.0, ((1, 16),), jnp.float32)
    norm_gain = jnp.clip(1.0 + 0.18 * jax.random.normal(splits[9], (D,), jnp.float32), 0.1, 1.9)
    out_sectioned = gaussian(splits[10], (H * DH, D), (H * DH) ** -0.5, 0.0625, ((0, 16), (1, 2)))
    expert_sectioned = gaussian(splits[11], (EXPERTS, D, 3, FFE), (D // 2) ** -0.5, 0.09375, ((0, 16), (1, 2)))
    bucket_owner = jax.vmap(lambda own: jax.random.permutation(own, N_REP))(jax.random.split(splits[12], EXPERTS)).reshape((EXPERTS, N_REP)).astype(jnp.int32)
    return {"hidden_in": hidden_in, "queries": queries, "new_keys": new_keys, "new_values": new_values, "cache_keys": cache_keys, "cache_values": cache_values, "cache_lengths": cache_lengths, "expert_ids": expert_ids, "router_logits": router_logits, "norm_gain": norm_gain, "out_sectioned": out_sectioned, "expert_sectioned": expert_sectioned, "bucket_owner": bucket_owner}


ROUTE_SCALE = 2.827
EPSILON = 1e-06

def attention(query_rows, key_cache, value_cache, fresh_keys, fresh_values, row_lengths, step_index):
    row_count, feature_count = query_rows.shape
    head_count = feature_count // DH
    cached = key_cache.shape[1]
    step_count = fresh_keys.shape[0]
    query_heads = query_rows.reshape(row_count, head_count, DH).astype(jnp.float32)
    keys_old = key_cache.reshape(row_count, cached, head_count, DH).astype(jnp.float32)
    values_old = value_cache.reshape(row_count, cached, head_count, DH).astype(jnp.float32)
    keys_recent = fresh_keys.reshape(step_count, row_count, head_count, DH).astype(jnp.float32)
    values_recent = fresh_values.reshape(step_count, row_count, head_count, DH).astype(jnp.float32)
    factor = 1.0 / math.sqrt(DH)
    scores_old = jnp.einsum('rhd,rchd->rhc', query_heads, keys_old) * factor
    in_cache = jnp.arange(cached, dtype=jnp.int32)[None, :] < row_lengths[:, None]
    scores_old = jnp.where(in_cache[:, None, :], scores_old, -1e+30)
    scores_recent = jnp.einsum('rhd,srhd->rhs', query_heads, keys_recent) * factor
    visible = jnp.arange(step_count, dtype=jnp.int32) <= step_index
    scores_recent = jnp.where(visible[None, None, :], scores_recent, -1e+30)
    scores = jnp.concatenate([scores_old, scores_recent], axis=2)
    largest = lax.optimization_barrier(jnp.max(scores, axis=2, keepdims=True))
    expsum = jnp.exp(scores - largest)
    denominator = lax.optimization_barrier(jnp.sum(expsum, axis=2))
    probs = lax.optimization_barrier(expsum.astype(jnp.bfloat16)).astype(jnp.float32)
    weighted = jnp.einsum('rhc,rchd->rhd', probs[:, :, :cached], values_old)
    weighted = weighted + jnp.einsum('rhs,srhd->rhd', probs[:, :, cached:], values_recent)
    return (weighted / denominator[:, :, None]).astype(jnp.bfloat16).reshape(row_count, feature_count)

def reference(hidden_in, queries, new_keys, new_values, cache_keys, cache_values, cache_lengths, expert_ids, router_logits, norm_gain, out_sectioned, expert_sectioned, bucket_owner):
    head_list = [attention(queries[step_index], cache_keys, cache_values, new_keys, new_values, cache_lengths, step_index) for step_index in range(STEPS)]
    head_matrix = jnp.stack(head_list).reshape(STEPS * ROWS, H * DH)
    group_width = H * DH // N_EP

    def add_group(running, offset):
        rows_part = lax.dynamic_slice_in_dim(head_matrix, offset, group_width, 1)
        weight_part = lax.dynamic_slice_in_dim(out_sectioned, offset, group_width, 0)
        term = jnp.dot(rows_part, weight_part, preferred_element_type=jnp.float32)
        rounded = lax.optimization_barrier(term.astype(jnp.bfloat16))
        return (running + rounded.astype(jnp.float32), None)
    offsets = (jnp.arange(N_EP, dtype=jnp.int32) * group_width).astype(jnp.int32)
    summed, unused = lax.scan(add_group, jnp.zeros((STEPS * ROWS, D), jnp.float32), offsets)
    attended = summed.astype(jnp.bfloat16).reshape(STEPS, ROWS, D)
    residual = hidden_in.astype(jnp.float32) + attended.astype(jnp.float32)
    mean_square = lax.optimization_barrier(jnp.mean(residual * residual, axis=2, keepdims=True))
    normalized = (residual * lax.rsqrt(mean_square + EPSILON) * norm_gain).astype(jnp.bfloat16)
    row_block = ROWS // N_EP
    chosen = expert_ids.reshape(STEPS, N_EP, row_block * TOPK)
    one_hot = (chosen[..., None] == jnp.arange(EXPERTS, dtype=jnp.int32)).astype(jnp.int32)
    earlier_count = lax.optimization_barrier(jnp.sum((jnp.cumsum(one_hot, axis=2) - one_hot) * one_hot, axis=3))
    per_expert = N_EP * STEPS * CAP
    device_offset = jnp.arange(N_EP, dtype=jnp.int32)[None, :, None] * (STEPS * CAP)
    step_offset = jnp.arange(STEPS, dtype=jnp.int32)[:, None, None] * CAP
    slot_order = (chosen * per_expert + device_offset + step_offset + earlier_count).reshape(-1).astype(jnp.int32)
    repeated = jnp.repeat(normalized.reshape(STEPS * ROWS, D), TOPK, axis=0)
    buffer_rows = jnp.zeros((EXPERTS * per_expert, D), jnp.bfloat16).at[slot_order].set(repeated)

    def expert_output(operands):
        block_rows, sectioned, owners = operands
        row_blocks = sectioned.reshape(N_REP, D // N_REP, 3, FFE)
        weight = jnp.take(row_blocks, owners, axis=0).reshape(D, 3, FFE)
        gate_value = jnp.dot(block_rows, weight[:, 0], preferred_element_type=jnp.float32)
        up_value = jnp.dot(block_rows, weight[:, 1], preferred_element_type=jnp.float32)
        activated = (jax.nn.silu(gate_value) * up_value).astype(jnp.bfloat16)
        return jnp.dot(activated, weight[:, 2].T, preferred_element_type=jnp.float32).astype(jnp.bfloat16)
    outputs = lax.map(expert_output, (buffer_rows.reshape(EXPERTS, per_expert, D), expert_sectioned, bucket_owner))
    picked = outputs.reshape(EXPERTS * per_expert, D)[slot_order].astype(jnp.float32).reshape(STEPS, ROWS, TOPK, D)
    affinity = jax.nn.sigmoid(router_logits)
    gate_share = ROUTE_SCALE * affinity / lax.optimization_barrier(jnp.sum(affinity, axis=2, keepdims=True))
    routed = lax.optimization_barrier(jnp.sum(gate_share[..., None] * picked, axis=2))
    return (residual + routed).astype(jnp.bfloat16)
```

```python
import math

import jax
import jax.numpy as jnp
from jax import lax
from jax.sharding import PartitionSpec as P

DH = 128
ROUTE_SCALE = 2.827
EPSILON = 1e-06


def attention(queries, new_keys, new_values, cache_keys, cache_values, cache_lengths):
    steps, rows, features = queries.shape
    heads = features // DH
    cached = cache_keys.shape[1]
    q = queries.reshape(steps, rows, heads, DH)
    keys_old = cache_keys.reshape(rows, cached, heads, DH)
    values_old = cache_values.reshape(rows, cached, heads, DH)
    keys_new = new_keys.reshape(steps, rows, heads, DH)
    values_new = new_values.reshape(steps, rows, heads, DH)
    factor = 1.0 / math.sqrt(DH)
    f32 = jnp.float32
    old = jnp.einsum("trhd,rchd->rhtc", q, keys_old, preferred_element_type=f32) * factor
    in_cache = jnp.arange(cached, dtype=jnp.int32)[None, :] < cache_lengths[:, None]
    old = jnp.where(in_cache[:, None, None, :], old, -1e30)
    new = jnp.einsum("trhd,srhd->rhts", q, keys_new, preferred_element_type=f32) * factor
    order = jnp.arange(steps, dtype=jnp.int32)
    new = jnp.where((order[None, :] <= order[:, None])[None, None], new, -1e30)
    largest = jnp.maximum(jnp.max(old, axis=3, keepdims=True), jnp.max(new, axis=3, keepdims=True))
    old = jnp.exp(old - largest)
    new = jnp.exp(new - largest)
    total = jnp.sum(old, axis=3) + jnp.sum(new, axis=3)
    weighted = jnp.einsum(
        "rhtc,rchd->rhtd", old.astype(jnp.bfloat16), values_old, preferred_element_type=f32
    ) + jnp.einsum(
        "rhts,srhd->rhtd", new.astype(jnp.bfloat16), values_new, preferred_element_type=f32
    )
    out = (weighted / total[..., None]).astype(jnp.bfloat16)
    return out.transpose(0, 2, 1, 3).reshape(rows, steps, features)


def on_device(
    hidden_in,
    queries,
    new_keys,
    new_values,
    cache_keys,
    cache_values,
    cache_lengths,
    expert_ids,
    router_logits,
    norm_gain,
    out_sectioned,
    expert_sectioned,
    bucket_owner,
):
    steps, row_block, width = hidden_in.shape
    n_ep = lax.axis_size("ep")
    n_rep = lax.axis_size("rep")
    me_rep = lax.axis_index("rep")
    me_ep = lax.axis_index("ep")
    half = width // n_rep
    own = steps * row_block
    part = own // n_rep
    f32, bf16 = jnp.float32, jnp.bfloat16
    owners = bucket_owner[0]
    bucket_of = jnp.argsort(owners)

    affinity = jax.nn.sigmoid(router_logits)
    share = ROUTE_SCALE * affinity / jnp.sum(affinity, axis=2, keepdims=True)
    experts = jnp.arange(n_ep, dtype=jnp.int32)
    dense = jnp.sum(jnp.where(expert_ids[..., None] == experts, share[..., None], 0.0), axis=2)
    dense = dense.transpose(1, 0, 2).reshape(own, n_ep)
    mix = lax.all_gather(dense, "ep", axis=0, tiled=False)
    mix = lax.dynamic_index_in_dim(mix, me_ep, axis=2, keepdims=False)
    mix = mix.reshape(n_ep, n_rep, part).transpose(1, 0, 2).reshape(-1, 1)

    heads = attention(queries, new_keys, new_values, cache_keys, cache_values, cache_lengths)
    heads = heads.reshape(n_ep * own, -1)
    partial = jnp.dot(heads, out_sectioned, preferred_element_type=f32).astype(bf16)
    summed = lax.psum_scatter(partial, "ep", scatter_dimension=0, tiled=True)
    swapped = lax.all_to_all(
        summed.reshape(n_rep, part, half), "rep", split_axis=0, concat_axis=0, tiled=True
    )
    attended = swapped.transpose(1, 0, 2).reshape(part, width)
    hidden = hidden_in.transpose(1, 0, 2).reshape(own, width)
    hidden = lax.dynamic_slice_in_dim(hidden, me_rep * part, part, 0)
    residual = hidden.astype(f32) + attended.astype(f32)
    mean_square = jnp.mean(residual * residual, axis=1, keepdims=True)
    normalized = (residual * lax.rsqrt(mean_square + EPSILON) * norm_gain).astype(bf16)

    gathered = lax.all_gather(normalized, "ep", axis=0, tiled=True)
    blocks = gathered.reshape(n_ep * part, n_rep, half).transpose(1, 0, 2)
    blocks = jnp.take(blocks, bucket_of, axis=0)
    arrived = lax.all_to_all(blocks, "rep", split_axis=0, concat_axis=0, tiled=True)
    arrived = arrived.reshape(n_rep * n_ep * part, half)

    weights = expert_sectioned[0]
    gate = jnp.dot(arrived, weights[:, 0], preferred_element_type=f32).astype(bf16)
    up = jnp.dot(arrived, weights[:, 1], preferred_element_type=f32).astype(bf16)
    both = jnp.stack([gate, up])
    both = lax.psum_scatter(both, "rep", scatter_dimension=1, tiled=True).astype(f32)
    activated = (jax.nn.silu(both[0]) * both[1]).astype(bf16)
    activated = lax.all_gather(activated, "rep", axis=0, tiled=True)
    out = jnp.einsum("nf,df->nd", activated, weights[:, 2], preferred_element_type=f32)
    out = (out * mix).astype(bf16)

    back = lax.all_to_all(
        out.reshape(n_rep, n_ep * part, half), "rep", split_axis=0, concat_axis=0, tiled=True
    )
    back = jnp.take(back, owners, axis=0).transpose(1, 0, 2).reshape(n_ep * part, width)
    routed = lax.psum_scatter(back, "ep", scatter_dimension=0, tiled=True)
    layer = (residual + routed.astype(f32)).astype(bf16)
    layer = lax.all_gather(layer, "rep", axis=0, tiled=True)
    return layer.reshape(row_block, steps, width).transpose(1, 0, 2)


def solution(mesh):
    return jax.shard_map(
        on_device,
        mesh=mesh,
        in_specs=(
            P(None, "ep", None),
            P(None, None, "ep"),
            P(None, None, "ep"),
            P(None, None, "ep"),
            P(None, None, "ep"),
            P(None, None, "ep"),
            P(),
            P(None, "ep", None),
            P(None, "ep", None),
            P(),
            P("ep", "rep"),
            P("ep", "rep", None, None),
            P("ep", None),
        ),
        out_specs=P(None, "ep", None),
        check_vma=False,
    )
```

```python
import functools
import math

import jax
import jax.numpy as jnp
from jax import lax
from jax.experimental import pallas as pl
from jax.experimental.pallas import tpu as pltpu
from jax.sharding import PartitionSpec as P

DH = 128
ROUTE_SCALE = 2.827
EPSILON = 1e-06
MESH = pl.DeviceIdType.MESH
VMEM_BYTES = 48 * 1024 * 1024


def attention(queries, new_keys, new_values, cache_keys, cache_values, cache_lengths):
    steps, rows, features = queries.shape
    heads = features // DH
    cached = cache_keys.shape[1]
    q = queries.reshape(steps, rows, heads, DH)
    keys_old = cache_keys.reshape(rows, cached, heads, DH)
    values_old = cache_values.reshape(rows, cached, heads, DH)
    keys_new = new_keys.reshape(steps, rows, heads, DH)
    values_new = new_values.reshape(steps, rows, heads, DH)
    factor = 1.0 / math.sqrt(DH)
    f32 = jnp.float32
    old = jnp.einsum("trhd,rchd->rhtc", q, keys_old, preferred_element_type=f32) * factor
    in_cache = jnp.arange(cached, dtype=jnp.int32)[None, :] < cache_lengths[:, None]
    old = jnp.where(in_cache[:, None, None, :], old, -1e30)
    new = jnp.einsum("trhd,srhd->rhts", q, keys_new, preferred_element_type=f32) * factor
    order = jnp.arange(steps, dtype=jnp.int32)
    new = jnp.where((order[None, :] <= order[:, None])[None, None], new, -1e30)
    largest = jnp.maximum(jnp.max(old, axis=3, keepdims=True), jnp.max(new, axis=3, keepdims=True))
    old = jnp.exp(old - largest)
    new = jnp.exp(new - largest)
    total = jnp.sum(old, axis=3) + jnp.sum(new, axis=3)
    weighted = jnp.einsum(
        "rhtc,rchd->rhtd", old.astype(jnp.bfloat16), values_old, preferred_element_type=f32
    ) + jnp.einsum(
        "rhts,srhd->rhtd", new.astype(jnp.bfloat16), values_new, preferred_element_type=f32
    )
    out = (weighted / total[..., None]).astype(jnp.bfloat16)
    return out.transpose(0, 2, 1, 3).reshape(rows, steps, features)


def place(n_ep):
    rep = lax.axis_index("rep")
    ep = lax.axis_index("ep")
    return rep, ep // 4, (ep // 2) % 2, ep % 2


def neighbours(n_far, rep, far, near, core):
    def at(rep_, far_, near_, core_):
        return (rep_, far_ * 4 + near_ * 2 + core_)

    others = [lax.rem(far + d, n_far) for d in range(1, n_far)]
    return (
        at(1 - rep, far, near, core),
        at(rep, far, near, 1 - core),
        at(rep, far, 1 - near, core),
        others,
        [at(rep, other, near, core) for other in others],
    )


def greet(devices):
    barrier = pltpu.get_barrier_semaphore()
    for device in devices:
        pl.semaphore_signal(barrier, inc=1, device_id=device, device_id_type=MESH)
    pl.semaphore_wait(barrier, len(devices))


def send(src, dst, sems, index, device):
    copy = pltpu.make_async_remote_copy(
        src_ref=src,
        dst_ref=dst,
        send_sem=sems.at[(0,) + index],
        recv_sem=sems.at[(1,) + index],
        device_id=device,
        device_id_type=MESH,
    )
    copy.start()
    return copy


def add_rows(x, y):
    return (x.astype(jnp.float32) + y.astype(jnp.float32)).astype(jnp.bfloat16)


class Scatter:
    def __init__(self, spot, links, source, from_core, half, from_near, quarter, from_far, sems):
        _, self.far, self.near, self.core = spot
        _, self.to_core, self.to_near, self.others, self.to_far = links
        self.source, self.from_core, self.half = source, from_core, half
        self.from_near, self.quarter, self.from_far = from_near, quarter, from_far
        self.sems = sems
        self.n_far = quarter.shape[1]

    def first(self, k):
        return send(
            self.source.at[k, :, 1 - self.core], self.from_core.at[k], self.sems, (k, 0),
            self.to_core,
        )

    def second(self, k):
        def add(j, _):
            self.half[k, j // 2, j % 2] = add_rows(
                self.source[k, j, self.core], self.from_core[k, j]
            )
            return 0

        lax.fori_loop(0, 2 * self.n_far, add, 0)
        return send(
            self.half.at[k, :, 1 - self.near], self.from_near.at[k], self.sems, (k, 1),
            self.to_near,
        )

    def third(self, k):
        def add(j, _):
            self.quarter[k, j] = add_rows(self.half[k, j, self.near], self.from_near[k, j])
            return 0

        lax.fori_loop(0, self.n_far, add, 0)
        return [
            send(self.quarter.at[k, other], self.from_far.at[k, d], self.sems, (k, 2 + d), device)
            for d, (other, device) in enumerate(zip(self.others, self.to_far))
        ]

    def total(self, k):
        total = self.quarter[k, self.far].astype(jnp.float32)
        for d in range(self.n_far - 1):
            total += self.from_far[k, d].astype(jnp.float32)
        return total


def scatter_scratch(n_far, chunks, block):
    bf16 = jnp.bfloat16
    return [
        pltpu.VMEM((chunks, 2 * n_far, 2) + block, bf16),
        pltpu.VMEM((chunks, 2 * n_far) + block, bf16),
        pltpu.VMEM((chunks, n_far, 2) + block, bf16),
        pltpu.VMEM((chunks, n_far) + block, bf16),
        pltpu.VMEM((chunks, n_far) + block, bf16),
        pltpu.VMEM((chunks, n_far - 1) + block, bf16),
        pltpu.SemaphoreType.DMA((2, chunks, n_far + 1)),
    ]


def dispatch_kernel(
    n_far,
    flag_ref,
    heads_ref,
    proj_ref,
    hidden_ref,
    gain_ref,
    rows_ref,
    residual_ref,
    source,
    from_core,
    half,
    from_near,
    quarter,
    from_far,
    sems,
    attended,
    gathered,
    staged,
    swap_sems,
    ring_sems,
    cross_sems,
):
    f32, bf16 = jnp.float32, jnp.bfloat16
    spot = rep, far, near, core = place(4 * n_far)
    links = to_rep, to_core, to_near, others, to_far = neighbours(n_far, *spot)
    greet([to_rep, to_core, to_near] + to_far)
    scatter = Scatter(
        spot, links, source, from_core, half, from_near, quarter, from_far, sems
    )
    own, piece = attended.shape[2], attended.shape[3]
    width = 4 * piece

    first = []
    for k in range(2):
        product = jnp.dot(
            heads_ref[...], proj_ref[:, k * piece : (k + 1) * piece], preferred_element_type=f32
        )
        source[k] = product.astype(bf16).reshape(2 * n_far, 2, own, piece)
        first.append(scatter.first(k))
    second = []
    for k in range(2):
        first[k].wait()
        second.append(scatter.second(k))
    third = []
    for k in range(2):
        second[k].wait()
        third.append(scatter.third(k))
    swaps = []
    for k in range(2):
        for copy in third[k]:
            copy.wait()
        attended[rep, k] = scatter.total(k).astype(bf16)
        swaps.append(
            send(attended.at[rep, k], attended.at[rep, k], swap_sems, (k,), to_rep)
        )
    for copy in swaps:
        copy.wait()

    squares = jnp.zeros((own, 1), f32)
    for h in range(2):
        for k in range(2):
            start = (2 * h + k) * piece
            residual = hidden_ref[:, start : start + piece].astype(f32)
            residual += attended[h, k].astype(f32)
            squares += jnp.sum(residual * residual, axis=1, keepdims=True)
    scale = lax.rsqrt(squares / width + EPSILON)
    for h in range(2):
        lanes = pl.ds(pl.multiple_of((2 * h + rep) * piece, 128), piece)
        residual = hidden_ref[:, lanes].astype(f32) + attended[h, rep].astype(f32)
        residual_ref[h] = residual
        gathered[far, near, core, h] = (residual * scale * gain_ref[:, lanes]).astype(bf16)

    flag = flag_ref[0, 0]
    mine = pl.ds(pl.multiple_of(rep * piece, 128), piece)
    pending = []

    def cross(f, n, c, index):
        low, high = gathered[f, n, c, 0], gathered[f, n, c, 1]
        rows_ref[f, n, c, :, mine] = jnp.where(flag == 0, low, high)
        staged[f, n, c] = jnp.where(flag == 0, high, low)
        pending.append(
            send(staged.at[f, n, c], rows_ref.at[f, n, c, :, mine], cross_sems, (index,), to_rep)
        )

    def pass_on(f, n, c, index, device):
        block = gathered.at[f, n, c]
        return send(block, block, ring_sems, (index,), device)

    far_copies = [
        pass_on(far, near, core, d, device) for d, device in enumerate(to_far)
    ]
    base = n_far - 1
    for d in range(n_far):
        behind = lax.rem(far + n_far - d, n_far)
        if d > 0:
            far_copies[d - 1].wait_recv()
        near_copy = pass_on(behind, near, core, base + 3 * d, to_near)
        core_copy = pass_on(behind, near, core, base + 3 * d + 1, to_core)
        cross(behind, near, core, 4 * d)
        near_copy.wait_recv()
        other_copy = pass_on(behind, 1 - near, core, base + 3 * d + 2, to_core)
        cross(behind, 1 - near, core, 4 * d + 1)
        core_copy.wait_recv()
        cross(behind, near, 1 - core, 4 * d + 2)
        other_copy.wait_recv()
        cross(behind, 1 - near, 1 - core, 4 * d + 3)
        near_copy.wait_send()
        core_copy.wait_send()
        other_copy.wait_send()
    for copy in far_copies:
        copy.wait_send()
    for copy in pending:
        copy.wait()


def dispatch(n_ep, flag, heads, projection, hidden, gain):
    n_far = n_ep // 4
    own, width = hidden.shape
    piece = width // 4
    bf16 = jnp.bfloat16
    vmem = pl.BlockSpec(memory_space=pltpu.VMEM)
    return pl.pallas_call(
        functools.partial(dispatch_kernel, n_far),
        out_shape=(
            jax.ShapeDtypeStruct((n_far, 2, 2, own, 2 * piece), bf16),
            jax.ShapeDtypeStruct((2, own, piece), jnp.float32),
        ),
        in_specs=[pl.BlockSpec(memory_space=pltpu.SMEM)] + [vmem] * 4,
        out_specs=(vmem, vmem),
        scratch_shapes=scatter_scratch(n_far, 2, (own, piece))
        + [
            pltpu.VMEM((2, 2, own, piece), bf16),
            pltpu.VMEM((n_far, 2, 2, 2, own, piece), bf16),
            pltpu.VMEM((n_far, 2, 2, own, piece), bf16),
            pltpu.SemaphoreType.DMA((2, 2)),
            pltpu.SemaphoreType.DMA((2, 4 * n_far - 1)),
            pltpu.SemaphoreType.DMA((2, 4 * n_far)),
        ],
        compiler_params=pltpu.CompilerParams(
            collective_id=0, has_side_effects=True, vmem_limit_bytes=VMEM_BYTES
        ),
    )(flag, heads, projection, hidden, gain)


def combine_kernel(
    n_far,
    flag_ref,
    out_ref,
    residual_ref,
    layer_ref,
    source,
    from_core,
    half,
    from_near,
    quarter,
    from_far,
    sems,
    from_rep,
    cross_sems,
    last_sems,
):
    spot = rep, far, near, core = place(4 * n_far)
    links = to_rep, to_core, to_near, others, to_far = neighbours(n_far, *spot)
    greet([to_rep, to_core, to_near] + to_far)
    scatter = Scatter(
        spot, links, source, from_core, half, from_near, quarter, from_far, sems
    )
    piece = residual_ref.shape[2]
    chunk = piece // 2
    flag = flag_ref[0, 0]

    def lanes(owner, k):
        return pl.ds(pl.multiple_of(owner * piece + k * chunk, 128), chunk)

    crossing = [
        send(out_ref.at[:, :, :, lanes(1 - rep, k)], from_rep.at[k], cross_sems, (k,), to_rep)
        for k in range(2)
    ]
    first = []
    for k in range(2):
        crossing[k].wait()

        def arrange(j, _):
            mine = out_ref[j // 2, j % 2, :, lanes(rep, k)]
            other = from_rep[k, j // 2, j % 2]
            source[k, j // 2, j % 2, 0] = jnp.where(flag == 0, mine, other)
            source[k, j // 2, j % 2, 1] = jnp.where(flag == 0, other, mine)
            return 0

        lax.fori_loop(0, 4 * n_far, arrange, 0)
        first.append(scatter.first(k))
        if k == 0:
            first[0].wait()
            second = [scatter.second(0)]
    second[0].wait()
    third = [scatter.third(0)]
    first[1].wait()
    second.append(scatter.second(1))
    second[1].wait()
    third.append(scatter.third(1))
    last = []
    for k in range(2):
        for copy in third[k]:
            copy.wait()
        layer = residual_ref[:, :, k * chunk : (k + 1) * chunk] + scatter.total(k)
        layer = layer.astype(jnp.bfloat16)
        for h in range(2):
            spot_lanes = pl.ds(
                pl.multiple_of((2 * h + rep) * piece + k * chunk, 128), chunk
            )
            layer_ref[:, spot_lanes] = layer[h]
            block = layer_ref.at[:, spot_lanes]
            last.append(send(block, block, last_sems, (2 * k + h,), to_rep))
    for copy in last:
        copy.wait()


def combine(n_ep, flag, out, residual):
    n_far = n_ep // 4
    _, own, piece = residual.shape
    bf16 = jnp.bfloat16
    vmem = pl.BlockSpec(memory_space=pltpu.VMEM)
    return pl.pallas_call(
        functools.partial(combine_kernel, n_far),
        out_shape=jax.ShapeDtypeStruct((own, 4 * piece), bf16),
        in_specs=[pl.BlockSpec(memory_space=pltpu.SMEM)] + [vmem] * 2,
        out_specs=vmem,
        scratch_shapes=scatter_scratch(n_far, 2, (2, own, piece // 2))
        + [
            pltpu.VMEM((2, 2 * n_far, 2, own, piece // 2), bf16),
            pltpu.SemaphoreType.DMA((2, 2)),
            pltpu.SemaphoreType.DMA((2, 4)),
        ],
        compiler_params=pltpu.CompilerParams(
            collective_id=1, has_side_effects=True, vmem_limit_bytes=VMEM_BYTES
        ),
    )(flag, out.reshape(2 * n_far, 2, own, 2 * piece), residual)


def on_device(
    hidden_in,
    queries,
    new_keys,
    new_values,
    cache_keys,
    cache_values,
    cache_lengths,
    expert_ids,
    router_logits,
    norm_gain,
    out_sectioned,
    expert_sectioned,
    bucket_owner,
):
    steps, row_block, width = hidden_in.shape
    n_ep = lax.axis_size("ep")
    n_rep = lax.axis_size("rep")
    me_rep = lax.axis_index("rep")
    me_ep = lax.axis_index("ep")
    half = width // n_rep
    own = steps * row_block
    part = own // n_rep
    f32, bf16 = jnp.float32, jnp.bfloat16
    owners = bucket_owner[0]
    bucket_of = jnp.argsort(owners)

    affinity = jax.nn.sigmoid(router_logits)
    share = ROUTE_SCALE * affinity / jnp.sum(affinity, axis=2, keepdims=True)
    experts = jnp.arange(n_ep, dtype=jnp.int32)
    dense = jnp.sum(jnp.where(expert_ids[..., None] == experts, share[..., None], 0.0), axis=2)
    dense = dense.transpose(1, 0, 2).reshape(own, n_ep)
    mix = lax.all_gather(dense, "ep", axis=0, tiled=False)
    mix = lax.dynamic_index_in_dim(mix, me_ep, axis=2, keepdims=False)

    heads = attention(queries, new_keys, new_values, cache_keys, cache_values, cache_lengths)
    heads = heads.reshape(n_ep * own, -1)
    hidden = hidden_in.transpose(1, 0, 2).reshape(own, width)
    by_kernel = n_rep == 2 and n_ep % 4 == 0 and own % 16 == 0 and half % 512 == 0
    if by_kernel:
        flag = (owners[0] != me_rep).astype(jnp.int32).reshape(1, 1)
        arrived, residual = dispatch(n_ep, flag, heads, out_sectioned, hidden, norm_gain[None])
        arrived = arrived.reshape(n_ep * own, half)
    else:
        partial = jnp.dot(heads, out_sectioned, preferred_element_type=f32).astype(bf16)
        summed = lax.psum_scatter(partial, "ep", scatter_dimension=0, tiled=True)
        swapped = lax.all_to_all(
            summed.reshape(n_rep, part, half), "rep", split_axis=0, concat_axis=0, tiled=True
        )
        attended = swapped.transpose(1, 0, 2).reshape(part, width)
        hidden = lax.dynamic_slice_in_dim(hidden, me_rep * part, part, 0)
        residual = hidden.astype(f32) + attended.astype(f32)
        mean_square = jnp.mean(residual * residual, axis=1, keepdims=True)
        normalized = (residual * lax.rsqrt(mean_square + EPSILON) * norm_gain).astype(bf16)

        gathered = lax.all_gather(normalized, "ep", axis=0, tiled=True)
        blocks = gathered.reshape(n_ep * part, n_rep, half).transpose(1, 0, 2)
        blocks = jnp.take(blocks, bucket_of, axis=0)
        arrived = lax.all_to_all(blocks, "rep", split_axis=0, concat_axis=0, tiled=True)
        arrived = arrived.reshape(n_rep * n_ep * part, half)

        mix = mix.reshape(n_ep, n_rep, part).transpose(1, 0, 2)
    mix = mix.reshape(-1, 1)

    weights = expert_sectioned[0]
    gate = jnp.dot(arrived, weights[:, 0], preferred_element_type=f32).astype(bf16)
    up = jnp.dot(arrived, weights[:, 1], preferred_element_type=f32).astype(bf16)
    both = jnp.stack([gate, up])
    both = lax.psum_scatter(both, "rep", scatter_dimension=1, tiled=True).astype(f32)
    activated = (jax.nn.silu(both[0]) * both[1]).astype(bf16)
    activated = lax.all_gather(activated, "rep", axis=0, tiled=True)
    out = jnp.einsum("nf,df->nd", activated, weights[:, 2], preferred_element_type=f32)
    out = (out * mix).astype(bf16)

    if by_kernel:
        layer = combine(n_ep, flag, out, residual)
        return layer.reshape(row_block, steps, width).transpose(1, 0, 2)
    back = lax.all_to_all(
        out.reshape(n_rep, n_ep * part, half), "rep", split_axis=0, concat_axis=0, tiled=True
    )
    back = jnp.take(back, owners, axis=0).transpose(1, 0, 2).reshape(n_ep * part, width)
    routed = lax.psum_scatter(back, "ep", scatter_dimension=0, tiled=True)
    layer = (residual + routed.astype(f32)).astype(bf16)
    layer = lax.all_gather(layer, "rep", axis=0, tiled=True)
    return layer.reshape(row_block, steps, width).transpose(1, 0, 2)


def solution(mesh):
    return jax.shard_map(
        on_device,
        mesh=mesh,
        in_specs=(
            P(None, "ep", None),
            P(None, None, "ep"),
            P(None, None, "ep"),
            P(None, None, "ep"),
            P(None, None, "ep"),
            P(None, None, "ep"),
            P(),
            P(None, "ep", None),
            P(None, "ep", None),
            P(),
            P("ep", "rep"),
            P("ep", "rep", None, None),
            P("ep", None),
        ),
        out_specs=P(None, "ep", None),
        check_vma=False,
    )
```

```python
import functools
import math

import jax
import jax.numpy as jnp
from jax import lax
from jax.experimental import pallas as pl
from jax.experimental.pallas import tpu as pltpu
from jax.sharding import PartitionSpec as P

DH = 128
ROUTE_SCALE = 2.827
EPSILON = 1e-06
MESH = pl.DeviceIdType.MESH
VMEM_BYTES = 60 * 1024 * 1024


def attention(queries, new_keys, new_values, cache_keys, cache_values, cache_lengths):
    steps, rows, features = queries.shape
    heads = features // DH
    cached = cache_keys.shape[1]
    q = queries.reshape(steps, rows, heads, DH)
    keys_old = cache_keys.reshape(rows, cached, heads, DH)
    values_old = cache_values.reshape(rows, cached, heads, DH)
    keys_new = new_keys.reshape(steps, rows, heads, DH)
    values_new = new_values.reshape(steps, rows, heads, DH)
    factor = 1.0 / math.sqrt(DH)
    f32 = jnp.float32
    old = jnp.einsum("trhd,rchd->rhtc", q, keys_old, preferred_element_type=f32) * factor
    in_cache = jnp.arange(cached, dtype=jnp.int32)[None, :] < cache_lengths[:, None]
    old = jnp.where(in_cache[:, None, None, :], old, -1e30)
    new = jnp.einsum("trhd,srhd->rhts", q, keys_new, preferred_element_type=f32) * factor
    order = jnp.arange(steps, dtype=jnp.int32)
    new = jnp.where((order[None, :] <= order[:, None])[None, None], new, -1e30)
    largest = jnp.maximum(jnp.max(old, axis=3, keepdims=True), jnp.max(new, axis=3, keepdims=True))
    old = jnp.exp(old - largest)
    new = jnp.exp(new - largest)
    total = jnp.sum(old, axis=3) + jnp.sum(new, axis=3)
    weighted = jnp.einsum(
        "rhtc,rchd->rhtd", old.astype(jnp.bfloat16), values_old, preferred_element_type=f32
    ) + jnp.einsum(
        "rhts,srhd->rhtd", new.astype(jnp.bfloat16), values_new, preferred_element_type=f32
    )
    out = (weighted / total[..., None]).astype(jnp.bfloat16)
    return out.transpose(0, 2, 1, 3).reshape(rows, steps, features)


def place(n_ep):
    rep = lax.axis_index("rep")
    ep = lax.axis_index("ep")
    return rep, ep // 4, (ep // 2) % 2, ep % 2


def neighbours(n_far, rep, far, near, core):
    def at(rep_, far_, near_, core_):
        return (rep_, far_ * 4 + near_ * 2 + core_)

    others = [lax.rem(far + d, n_far) for d in range(1, n_far)]
    return (
        at(1 - rep, far, near, core),
        at(rep, far, near, 1 - core),
        at(rep, far, 1 - near, core),
        others,
        [at(rep, other, near, core) for other in others],
    )


def greet(devices):
    barrier = pltpu.get_barrier_semaphore()
    for device in devices:
        pl.semaphore_signal(barrier, inc=1, device_id=device, device_id_type=MESH)
    pl.semaphore_wait(barrier, len(devices))


def send(src, dst, sems, index, device):
    copy = pltpu.make_async_remote_copy(
        src_ref=src,
        dst_ref=dst,
        send_sem=sems.at[(0,) + index],
        recv_sem=sems.at[(1,) + index],
        device_id=device,
        device_id_type=MESH,
    )
    copy.start()
    return copy


def add_rows(x, y):
    return (x.astype(jnp.float32) + y.astype(jnp.float32)).astype(jnp.bfloat16)


class Scatter:
    def __init__(self, spot, links, source, from_core, half, from_near, quarter, from_far, sems):
        _, self.far, self.near, self.core = spot
        _, self.to_core, self.to_near, self.others, self.to_far = links
        self.source, self.from_core, self.half = source, from_core, half
        self.from_near, self.quarter, self.from_far = from_near, quarter, from_far
        self.sems = sems
        self.n_far = quarter.shape[1]

    def first(self, k):
        return send(
            self.source.at[k, :, 1 - self.core], self.from_core.at[k], self.sems, (k, 0),
            self.to_core,
        )

    def second(self, k):
        def add(j, _):
            self.half[k, j // 2, j % 2] = add_rows(
                self.source[k, j, self.core], self.from_core[k, j]
            )
            return 0

        lax.fori_loop(0, 2 * self.n_far, add, 0)
        return send(
            self.half.at[k, :, 1 - self.near], self.from_near.at[k], self.sems, (k, 1),
            self.to_near,
        )

    def third(self, k):
        def add(j, _):
            self.quarter[k, j] = add_rows(self.half[k, j, self.near], self.from_near[k, j])
            return 0

        lax.fori_loop(0, self.n_far, add, 0)
        return [
            send(self.quarter.at[k, other], self.from_far.at[k, d], self.sems, (k, 2 + d), device)
            for d, (other, device) in enumerate(zip(self.others, self.to_far))
        ]

    def total(self, k):
        total = self.quarter[k, self.far].astype(jnp.float32)
        for d in range(self.n_far - 1):
            total += self.from_far[k, d].astype(jnp.float32)
        return total


def scatter_scratch(n_far, chunks, block):
    bf16 = jnp.bfloat16
    return [
        pltpu.VMEM((chunks, 2 * n_far, 2) + block, bf16),
        pltpu.VMEM((chunks, 2 * n_far) + block, bf16),
        pltpu.VMEM((chunks, n_far, 2) + block, bf16),
        pltpu.VMEM((chunks, n_far) + block, bf16),
        pltpu.VMEM((chunks, n_far) + block, bf16),
        pltpu.VMEM((chunks, n_far - 1) + block, bf16),
        pltpu.SemaphoreType.DMA((2, chunks, n_far + 1)),
    ]


def layer_kernel(
    n_far,
    flag_ref,
    heads_ref,
    proj_ref,
    hidden_ref,
    gain_ref,
    mix_ref,
    weights_ref,
    layer_ref,
    source,
    from_core,
    half,
    from_near,
    quarter,
    from_far,
    sems,
    source2,
    from_core2,
    half2,
    from_near2,
    quarter2,
    from_far2,
    sems2,
    attended,
    residual_ref,
    gathered,
    staged,
    rows_ref,
    weights,
    hidden_sum,
    sent_sum,
    other_sum,
    activated,
    out_sum,
    out_ref,
    from_rep,
    weight_sems,
    swap_sems,
    ring_sems,
    cross_sems,
    sum_sems,
    active_sems,
    back_sems,
    last_sems,
):
    f32, bf16 = jnp.float32, jnp.bfloat16
    loads = [
        pltpu.make_async_copy(weights_ref.at[i], weights.at[i], weight_sems.at[i])
        for i in range(3)
    ]
    for load in loads:
        load.start()
    spot = rep, far, near, core = place(4 * n_far)
    links = to_rep, to_core, to_near, others, to_far = neighbours(n_far, *spot)
    greet([to_rep, to_core, to_near] + to_far)
    scatter = Scatter(spot, links, source, from_core, half, from_near, quarter, from_far, sems)
    own, piece = attended.shape[2], attended.shape[3]
    width = 4 * piece
    chunk = piece // 2
    count = 4 * n_far * own

    first = []
    for k in range(2):
        product = jnp.dot(
            heads_ref[...], proj_ref[:, k * piece : (k + 1) * piece], preferred_element_type=f32
        )
        source[k] = product.astype(bf16).reshape(2 * n_far, 2, own, piece)
        first.append(scatter.first(k))
    second = []
    for k in range(2):
        first[k].wait()
        second.append(scatter.second(k))
    third = []
    for k in range(2):
        second[k].wait()
        third.append(scatter.third(k))
    swaps = []
    for k in range(2):
        for copy in third[k]:
            copy.wait()
        attended[rep, k] = scatter.total(k).astype(bf16)
        swaps.append(send(attended.at[rep, k], attended.at[rep, k], swap_sems, (k,), to_rep))
    for copy in swaps:
        copy.wait()

    squares = jnp.zeros((own, 1), f32)
    for h in range(2):
        for k in range(2):
            start = (2 * h + k) * piece
            residual = hidden_ref[:, start : start + piece].astype(f32)
            residual += attended[h, k].astype(f32)
            squares += jnp.sum(residual * residual, axis=1, keepdims=True)
    scale = lax.rsqrt(squares / width + EPSILON)
    for h in range(2):
        lanes = pl.ds(pl.multiple_of((2 * h + rep) * piece, 128), piece)
        residual = hidden_ref[:, lanes].astype(f32) + attended[h, rep].astype(f32)
        residual_ref[h] = residual
        gathered[far, near, core, h] = (residual * scale * gain_ref[:, lanes]).astype(bf16)

    flag = flag_ref[0, 0]
    pending = []

    def cross(f, n, c, index):
        low, high = gathered[f, n, c, 0], gathered[f, n, c, 1]
        rows_ref[rep, f, n, c] = jnp.where(flag == 0, low, high)
        staged[f, n, c] = jnp.where(flag == 0, high, low)
        pending.append(
            send(staged.at[f, n, c], rows_ref.at[rep, f, n, c], cross_sems, (index,), to_rep)
        )

    def pass_on(f, n, c, index, device):
        block = gathered.at[f, n, c]
        return send(block, block, ring_sems, (index,), device)

    far_copies = [pass_on(far, near, core, d, device) for d, device in enumerate(to_far)]
    base = n_far - 1
    for d in range(n_far):
        behind = lax.rem(far + n_far - d, n_far)
        if d > 0:
            far_copies[d - 1].wait_recv()
        near_copy = pass_on(behind, near, core, base + 3 * d, to_near)
        core_copy = pass_on(behind, near, core, base + 3 * d + 1, to_core)
        cross(behind, near, core, 4 * d)
        near_copy.wait_recv()
        other_copy = pass_on(behind, 1 - near, core, base + 3 * d + 2, to_core)
        cross(behind, 1 - near, core, 4 * d + 1)
        core_copy.wait_recv()
        cross(behind, near, 1 - core, 4 * d + 2)
        other_copy.wait_recv()
        cross(behind, 1 - near, 1 - core, 4 * d + 3)
        near_copy.wait_send()
        core_copy.wait_send()
        other_copy.wait_send()
    for copy in far_copies:
        copy.wait_send()

    tile = hidden_sum.shape[2] // 2

    def products(q, t):
        x = rows_ref[q].reshape(count, piece)
        depth = pl.ds(pl.multiple_of(q * piece, 128), piece)
        lanes = pl.ds(pl.multiple_of(t * tile, 128), tile)
        gate = jnp.dot(x, weights[0, depth, lanes], preferred_element_type=f32)
        up = jnp.dot(x, weights[1, depth, lanes], preferred_element_type=f32)
        return gate, up

    loads[0].wait()
    loads[1].wait()

    def own_piece(t, _):
        gate, up = products(rep, t)
        hidden_sum[t, :, :tile] = gate
        hidden_sum[t, :, tile:] = up
        return 0

    lax.fori_loop(0, 4, own_piece, 0)
    for copy in pending:
        copy.wait()
    sums = []
    for i in range(2):
        t = 2 * (1 - rep) + i
        gate, up = products(1 - rep, t)
        sent_sum[i, :, :tile] = (hidden_sum[t, :, :tile] + gate).astype(bf16)
        sent_sum[i, :, tile:] = (hidden_sum[t, :, tile:] + up).astype(bf16)
        sums.append(send(sent_sum.at[i], other_sum.at[i], sum_sems, (i,), to_rep))

    def other_piece(i, _):
        t = 2 * rep + i
        gate, up = products(1 - rep, t)
        hidden_sum[t, :, :tile] += gate
        hidden_sum[t, :, tile:] += up
        return 0

    lax.fori_loop(0, 2, other_piece, 0)
    active = []
    for i in range(2):
        sums[i].wait()
        t = 2 * rep + i
        gate = hidden_sum[t, :, :tile] + other_sum[i, :, :tile].astype(f32)
        up = hidden_sum[t, :, tile:] + other_sum[i, :, tile:].astype(f32)
        activated[rep, i] = (gate / (1.0 + jnp.exp(-gate)) * up).astype(bf16)
        active.append(
            send(activated.at[rep, i], activated.at[rep, i], active_sems, (i,), to_rep)
        )

    def down(side, j):
        total = jnp.zeros((count, chunk), f32)
        for i in range(2):
            rows = pl.ds(pl.multiple_of(j * chunk, 128), chunk)
            lanes = pl.ds(pl.multiple_of((2 * side + i) * tile, 128), tile)
            total += lax.dot_general(
                activated[side, i],
                weights[2, rows, lanes],
                (((1,), (1,)), ((), ())),
                preferred_element_type=f32,
            )
        return total

    loads[2].wait()

    def own_hidden(j, _):
        out_sum[j] = down(rep, j)
        return 0

    lax.fori_loop(0, 4, own_hidden, 0)
    for copy in active:
        copy.wait()

    def finish(j):
        out = (out_sum[j] + down(1 - rep, j)) * mix_ref[...]
        out_ref[j] = out.astype(bf16).reshape(2 * n_far, 2, own, chunk)

    back = []
    for k in range(2):
        finish(2 * (1 - rep) + k)
        back.append(
            send(out_ref.at[2 * (1 - rep) + k], from_rep.at[k], back_sems, (k,), to_rep)
        )

    def finish_own(k, _):
        finish(2 * rep + k)
        return 0

    lax.fori_loop(0, 2, finish_own, 0)

    scatter = Scatter(
        spot, links, source2, from_core2, half2, from_near2, quarter2, from_far2, sems2
    )
    first = []
    for k in range(2):
        back[k].wait()

        def arrange(j, _):
            mine = out_ref[2 * rep + k, j // 2, j % 2]
            other = from_rep[k, j // 2, j % 2]
            source2[k, j // 2, j % 2, 0] = jnp.where(flag == 0, mine, other)
            source2[k, j // 2, j % 2, 1] = jnp.where(flag == 0, other, mine)
            return 0

        lax.fori_loop(0, 4 * n_far, arrange, 0)
        first.append(scatter.first(k))
        if k == 0:
            first[0].wait()
            second = [scatter.second(0)]
    second[0].wait()
    third = [scatter.third(0)]
    first[1].wait()
    second.append(scatter.second(1))
    second[1].wait()
    third.append(scatter.third(1))
    last = []
    for k in range(2):
        for copy in third[k]:
            copy.wait()
        layer = residual_ref[:, :, k * chunk : (k + 1) * chunk] + scatter.total(k)
        layer = layer.astype(bf16)
        for h in range(2):
            lanes = pl.ds(pl.multiple_of((2 * h + rep) * piece + k * chunk, 128), chunk)
            layer_ref[:, lanes] = layer[h]
            block = layer_ref.at[:, lanes]
            last.append(send(block, block, last_sems, (2 * k + h,), to_rep))
    for copy in last:
        copy.wait()


def layer(n_ep, flag, heads, projection, hidden, gain, mix, weights):
    n_far = n_ep // 4
    own, width = hidden.shape
    piece = width // 4
    chunk = piece // 2
    count = n_ep * own
    units = weights.shape[2]
    tile = units // 4
    f32, bf16 = jnp.float32, jnp.bfloat16
    vmem = pl.BlockSpec(memory_space=pltpu.VMEM)
    return pl.pallas_call(
        functools.partial(layer_kernel, n_far),
        out_shape=jax.ShapeDtypeStruct((own, width), bf16),
        in_specs=[pl.BlockSpec(memory_space=pltpu.SMEM)]
        + [vmem] * 5
        + [pl.BlockSpec(memory_space=pl.ANY)],
        out_specs=vmem,
        scratch_shapes=scatter_scratch(n_far, 2, (own, piece))
        + scatter_scratch(n_far, 2, (2, own, chunk))
        + [
            pltpu.VMEM((2, 2, own, piece), bf16),
            pltpu.VMEM((2, own, piece), f32),
            pltpu.VMEM((n_far, 2, 2, 2, own, piece), bf16),
            pltpu.VMEM((n_far, 2, 2, own, piece), bf16),
            pltpu.VMEM((2, n_far, 2, 2, own, piece), bf16),
            pltpu.VMEM(weights.shape, bf16),
            pltpu.VMEM((4, count, 2 * tile), f32),
            pltpu.VMEM((2, count, 2 * tile), bf16),
            pltpu.VMEM((2, count, 2 * tile), bf16),
            pltpu.VMEM((2, 2, count, tile), bf16),
            pltpu.VMEM((4, count, chunk), f32),
            pltpu.VMEM((4, 2 * n_far, 2, own, chunk), bf16),
            pltpu.VMEM((2, 2 * n_far, 2, own, chunk), bf16),
            pltpu.SemaphoreType.DMA((3,)),
            pltpu.SemaphoreType.DMA((2, 2)),
            pltpu.SemaphoreType.DMA((2, 4 * n_far - 1)),
            pltpu.SemaphoreType.DMA((2, 4 * n_far)),
            pltpu.SemaphoreType.DMA((2, 2)),
            pltpu.SemaphoreType.DMA((2, 2)),
            pltpu.SemaphoreType.DMA((2, 2)),
            pltpu.SemaphoreType.DMA((2, 4)),
        ],
        compiler_params=pltpu.CompilerParams(
            collective_id=0, has_side_effects=True, vmem_limit_bytes=VMEM_BYTES
        ),
    )(flag, heads, projection, hidden, gain, mix, weights)


def on_device(
    hidden_in,
    queries,
    new_keys,
    new_values,
    cache_keys,
    cache_values,
    cache_lengths,
    expert_ids,
    router_logits,
    norm_gain,
    out_sectioned,
    expert_sectioned,
    bucket_owner,
):
    steps, row_block, width = hidden_in.shape
    n_ep = lax.axis_size("ep")
    n_rep = lax.axis_size("rep")
    me_rep = lax.axis_index("rep")
    me_ep = lax.axis_index("ep")
    half = width // n_rep
    own = steps * row_block
    part = own // n_rep
    f32, bf16 = jnp.float32, jnp.bfloat16
    owners = bucket_owner[0]
    bucket_of = jnp.argsort(owners)

    affinity = jax.nn.sigmoid(router_logits)
    share = ROUTE_SCALE * affinity / jnp.sum(affinity, axis=2, keepdims=True)
    experts = jnp.arange(n_ep, dtype=jnp.int32)
    dense = jnp.sum(jnp.where(expert_ids[..., None] == experts, share[..., None], 0.0), axis=2)
    dense = dense.transpose(1, 0, 2).reshape(own, n_ep)
    mix = lax.all_gather(dense, "ep", axis=0, tiled=False)
    mix = lax.dynamic_index_in_dim(mix, me_ep, axis=2, keepdims=False)

    heads = attention(queries, new_keys, new_values, cache_keys, cache_values, cache_lengths)
    heads = heads.reshape(n_ep * own, -1)
    hidden = hidden_in.transpose(1, 0, 2).reshape(own, width)
    weights = expert_sectioned[0]
    by_kernel = n_rep == 2 and n_ep % 4 == 0 and own % 16 == 0 and half % 512 == 0
    if by_kernel and weights.shape[2] % 512 == 0:
        flag = (owners[0] != me_rep).astype(jnp.int32).reshape(1, 1)
        out = layer(
            n_ep,
            flag,
            heads,
            out_sectioned,
            hidden,
            norm_gain[None],
            mix.reshape(-1, 1),
            weights.transpose(1, 0, 2),
        )
        return out.reshape(row_block, steps, width).transpose(1, 0, 2)
    partial = jnp.dot(heads, out_sectioned, preferred_element_type=f32).astype(bf16)
    summed = lax.psum_scatter(partial, "ep", scatter_dimension=0, tiled=True)
    swapped = lax.all_to_all(
        summed.reshape(n_rep, part, half), "rep", split_axis=0, concat_axis=0, tiled=True
    )
    attended = swapped.transpose(1, 0, 2).reshape(part, width)
    hidden = lax.dynamic_slice_in_dim(hidden, me_rep * part, part, 0)
    residual = hidden.astype(f32) + attended.astype(f32)
    mean_square = jnp.mean(residual * residual, axis=1, keepdims=True)
    normalized = (residual * lax.rsqrt(mean_square + EPSILON) * norm_gain).astype(bf16)

    gathered = lax.all_gather(normalized, "ep", axis=0, tiled=True)
    blocks = gathered.reshape(n_ep * part, n_rep, half).transpose(1, 0, 2)
    blocks = jnp.take(blocks, bucket_of, axis=0)
    arrived = lax.all_to_all(blocks, "rep", split_axis=0, concat_axis=0, tiled=True)
    arrived = arrived.reshape(n_rep * n_ep * part, half)

    mix = mix.reshape(n_ep, n_rep, part).transpose(1, 0, 2)
    mix = mix.reshape(-1, 1)
    gate = jnp.dot(arrived, weights[:, 0], preferred_element_type=f32).astype(bf16)
    up = jnp.dot(arrived, weights[:, 1], preferred_element_type=f32).astype(bf16)
    both = jnp.stack([gate, up])
    both = lax.psum_scatter(both, "rep", scatter_dimension=1, tiled=True).astype(f32)
    activated = (jax.nn.silu(both[0]) * both[1]).astype(bf16)
    activated = lax.all_gather(activated, "rep", axis=0, tiled=True)
    out = jnp.einsum("nf,df->nd", activated, weights[:, 2], preferred_element_type=f32)
    out = (out * mix).astype(bf16)

    back = lax.all_to_all(
        out.reshape(n_rep, n_ep * part, half), "rep", split_axis=0, concat_axis=0, tiled=True
    )
    back = jnp.take(back, owners, axis=0).transpose(1, 0, 2).reshape(n_ep * part, width)
    routed = lax.psum_scatter(back, "ep", scatter_dimension=0, tiled=True)
    result = (residual + routed.astype(f32)).astype(bf16)
    result = lax.all_gather(result, "rep", axis=0, tiled=True)
    return result.reshape(row_block, steps, width).transpose(1, 0, 2)


def solution(mesh):
    return jax.shard_map(
        on_device,
        mesh=mesh,
        in_specs=(
            P(None, "ep", None),
            P(None, None, "ep"),
            P(None, None, "ep"),
            P(None, None, "ep"),
            P(None, None, "ep"),
            P(None, None, "ep"),
            P(),
            P(None, "ep", None),
            P(None, "ep", None),
            P(),
            P("ep", "rep"),
            P("ep", "rep", None, None),
            P("ep", None),
        ),
        out_specs=P(None, "ep", None),
        check_vma=False,
    )
```

```python
import functools
import math

import jax
import jax.numpy as jnp
from jax import lax
from jax.experimental import pallas as pl
from jax.experimental.pallas import tpu as pltpu
from jax.sharding import PartitionSpec as P

DH = 128
ROUTE_SCALE = 2.827
EPSILON = 1e-06
MESH = pl.DeviceIdType.MESH
VMEM_BYTES = 60 * 1024 * 1024


def attention(queries, new_keys, new_values, cache_keys, cache_values, cache_lengths):
    steps, rows, features = queries.shape
    heads = features // DH
    cached = cache_keys.shape[1]
    q = queries.reshape(steps, rows, heads, DH)
    keys_old = cache_keys.reshape(rows, cached, heads, DH)
    values_old = cache_values.reshape(rows, cached, heads, DH)
    keys_new = new_keys.reshape(steps, rows, heads, DH)
    values_new = new_values.reshape(steps, rows, heads, DH)
    factor = 1.0 / math.sqrt(DH)
    f32 = jnp.float32
    old = jnp.einsum("trhd,rchd->rhtc", q, keys_old, preferred_element_type=f32) * factor
    in_cache = jnp.arange(cached, dtype=jnp.int32)[None, :] < cache_lengths[:, None]
    old = jnp.where(in_cache[:, None, None, :], old, -1e30)
    new = jnp.einsum("trhd,srhd->rhts", q, keys_new, preferred_element_type=f32) * factor
    order = jnp.arange(steps, dtype=jnp.int32)
    new = jnp.where((order[None, :] <= order[:, None])[None, None], new, -1e30)
    largest = jnp.maximum(jnp.max(old, axis=3, keepdims=True), jnp.max(new, axis=3, keepdims=True))
    old = jnp.exp(old - largest)
    new = jnp.exp(new - largest)
    total = jnp.sum(old, axis=3) + jnp.sum(new, axis=3)
    weighted = jnp.einsum(
        "rhtc,rchd->rhtd", old.astype(jnp.bfloat16), values_old, preferred_element_type=f32
    ) + jnp.einsum(
        "rhts,srhd->rhtd", new.astype(jnp.bfloat16), values_new, preferred_element_type=f32
    )
    out = (weighted / total[..., None]).astype(jnp.bfloat16)
    return out.transpose(0, 2, 1, 3).reshape(rows, steps, features)


def place(n_ep):
    rep = lax.axis_index("rep")
    ep = lax.axis_index("ep")
    return rep, ep // 4, (ep // 2) % 2, ep % 2


def neighbours(n_far, rep, far, near, core):
    def at(rep_, far_, near_, core_):
        return (rep_, far_ * 4 + near_ * 2 + core_)

    others = [lax.rem(far + d, n_far) for d in range(1, n_far)]
    return (
        at(1 - rep, far, near, core),
        at(rep, far, near, 1 - core),
        at(rep, far, 1 - near, core),
        others,
        [at(rep, other, near, core) for other in others],
    )


def greet(devices):
    barrier = pltpu.get_barrier_semaphore()
    for device in devices:
        pl.semaphore_signal(barrier, inc=1, device_id=device, device_id_type=MESH)
    pl.semaphore_wait(barrier, len(devices))


def send(src, dst, sems, index, device):
    copy = pltpu.make_async_remote_copy(
        src_ref=src,
        dst_ref=dst,
        send_sem=sems.at[(0,) + index],
        recv_sem=sems.at[(1,) + index],
        device_id=device,
        device_id_type=MESH,
    )
    copy.start()
    return copy


def add_rows(x, y):
    return (x.astype(jnp.float32) + y.astype(jnp.float32)).astype(jnp.bfloat16)


class Scatter:
    def __init__(self, spot, links, source, from_core, half, from_near, quarter, from_far, sems):
        _, self.far, self.near, self.core = spot
        _, self.to_core, self.to_near, self.others, self.to_far = links
        self.source, self.from_core, self.half = source, from_core, half
        self.from_near, self.quarter, self.from_far = from_near, quarter, from_far
        self.sems = sems
        self.n_far = quarter.shape[1]

    def first(self, k):
        return send(
            self.source.at[k, :, 1 - self.core], self.from_core.at[k], self.sems, (k, 0),
            self.to_core,
        )

    def second(self, k):
        def add(j, _):
            self.half[k, j // 2, j % 2] = add_rows(
                self.source[k, j, self.core], self.from_core[k, j]
            )
            return 0

        lax.fori_loop(0, 2 * self.n_far, add, 0)
        return send(
            self.half.at[k, :, 1 - self.near], self.from_near.at[k], self.sems, (k, 1),
            self.to_near,
        )

    def third(self, k):
        def add(j, _):
            self.quarter[k, j] = add_rows(self.half[k, j, self.near], self.from_near[k, j])
            return 0

        lax.fori_loop(0, self.n_far, add, 0)
        return [
            send(self.quarter.at[k, other], self.from_far.at[k, d], self.sems, (k, 2 + d), device)
            for d, (other, device) in enumerate(zip(self.others, self.to_far))
        ]

    def total(self, k):
        total = self.quarter[k, self.far].astype(jnp.float32)
        for d in range(self.n_far - 1):
            total += self.from_far[k, d].astype(jnp.float32)
        return total


def scatter_scratch(n_far, chunks, block):
    bf16 = jnp.bfloat16
    return [
        pltpu.VMEM((chunks, 2 * n_far, 2) + block, bf16),
        pltpu.VMEM((chunks, 2 * n_far) + block, bf16),
        pltpu.VMEM((chunks, n_far, 2) + block, bf16),
        pltpu.VMEM((chunks, n_far) + block, bf16),
        pltpu.VMEM((chunks, n_far) + block, bf16),
        pltpu.VMEM((chunks, n_far - 1) + block, bf16),
        pltpu.SemaphoreType.DMA((2, chunks, n_far + 1)),
    ]


def layer_kernel(
    n_far,
    flag_ref,
    heads_ref,
    proj_ref,
    hidden_ref,
    gain_ref,
    share_ref,
    weights_ref,
    layer_ref,
    source,
    from_core,
    half,
    from_near,
    quarter,
    from_far,
    sems,
    source2,
    from_core2,
    half2,
    from_near2,
    quarter2,
    from_far2,
    sems2,
    attended,
    residual_ref,
    gathered,
    staged,
    rows_ref,
    weights,
    hidden_sum,
    sent_sum,
    other_sum,
    activated,
    out_sum,
    out_ref,
    from_rep,
    weight_sems,
    swap_sems,
    ring_sems,
    cross_sems,
    sum_sems,
    active_sems,
    back_sems,
    last_sems,
    shares,
    share_sems,
):
    f32, bf16 = jnp.float32, jnp.bfloat16
    loads = [
        pltpu.make_async_copy(weights_ref.at[i], weights.at[i], weight_sems.at[i])
        for i in range(3)
    ]
    for load in loads:
        load.start()
    spot = rep, far, near, core = place(4 * n_far)
    links = to_rep, to_core, to_near, others, to_far = neighbours(n_far, *spot)
    greet([to_rep, to_core, to_near] + to_far)
    scatter = Scatter(spot, links, source, from_core, half, from_near, quarter, from_far, sems)
    own, piece = attended.shape[2], attended.shape[3]
    width = 4 * piece
    chunk = piece // 2
    count = 4 * n_far * own

    shares[far, near, core] = share_ref[...]

    def pass_shares(index, device, block):
        return send(block, block, share_sems, (index,), device)

    share_far = [
        pass_shares(d, device, shares.at[far, near, core]) for d, device in enumerate(to_far)
    ]

    first = []
    for k in range(2):
        product = jnp.dot(
            heads_ref[...], proj_ref[:, k * piece : (k + 1) * piece], preferred_element_type=f32
        )
        source[k] = product.astype(bf16).reshape(2 * n_far, 2, own, piece)
        first.append(scatter.first(k))
    second = []
    for k in range(2):
        first[k].wait()
        second.append(scatter.second(k))
    for copy in share_far:
        copy.wait()
    share_near = pass_shares(n_far - 1, to_near, shares.at[:, near, core])
    third = []
    for k in range(2):
        second[k].wait()
        third.append(scatter.third(k))
    share_near.wait()
    share_core = pass_shares(n_far, to_core, shares.at[:, :, core])
    swaps = []
    for k in range(2):
        for copy in third[k]:
            copy.wait()
        attended[rep, k] = scatter.total(k).astype(bf16)
        swaps.append(send(attended.at[rep, k], attended.at[rep, k], swap_sems, (k,), to_rep))
    for copy in swaps:
        copy.wait()

    squares = jnp.zeros((own, 1), f32)
    for h in range(2):
        for k in range(2):
            start = (2 * h + k) * piece
            residual = hidden_ref[:, start : start + piece].astype(f32)
            residual += attended[h, k].astype(f32)
            squares += jnp.sum(residual * residual, axis=1, keepdims=True)
    scale = lax.rsqrt(squares / width + EPSILON)
    for h in range(2):
        lanes = pl.ds(pl.multiple_of((2 * h + rep) * piece, 128), piece)
        residual = hidden_ref[:, lanes].astype(f32) + attended[h, rep].astype(f32)
        residual_ref[h] = residual
        gathered[far, near, core, h] = (residual * scale * gain_ref[:, lanes]).astype(bf16)

    flag = flag_ref[0, 0]
    pending = []

    def cross(f, n, c, index):
        low, high = gathered[f, n, c, 0], gathered[f, n, c, 1]
        rows_ref[rep, f, n, c] = jnp.where(flag == 0, low, high)
        staged[f, n, c] = jnp.where(flag == 0, high, low)
        pending.append(
            send(staged.at[f, n, c], rows_ref.at[rep, f, n, c], cross_sems, (index,), to_rep)
        )

    def pass_on(f, n, c, index, device):
        block = gathered.at[f, n, c]
        return send(block, block, ring_sems, (index,), device)

    far_copies = [pass_on(far, near, core, d, device) for d, device in enumerate(to_far)]
    base = n_far - 1
    for d in range(n_far):
        behind = lax.rem(far + n_far - d, n_far)
        if d > 0:
            far_copies[d - 1].wait_recv()
        near_copy = pass_on(behind, near, core, base + 3 * d, to_near)
        core_copy = pass_on(behind, near, core, base + 3 * d + 1, to_core)
        cross(behind, near, core, 4 * d)
        near_copy.wait_recv()
        other_copy = pass_on(behind, 1 - near, core, base + 3 * d + 2, to_core)
        cross(behind, 1 - near, core, 4 * d + 1)
        core_copy.wait_recv()
        cross(behind, near, 1 - core, 4 * d + 2)
        other_copy.wait_recv()
        cross(behind, 1 - near, 1 - core, 4 * d + 3)
        near_copy.wait_send()
        core_copy.wait_send()
        other_copy.wait_send()
    for copy in far_copies:
        copy.wait_send()

    tile = hidden_sum.shape[2] // 2

    def products(q, t):
        x = rows_ref[q].reshape(count, piece)
        depth = pl.ds(pl.multiple_of(q * piece, 128), piece)
        lanes = pl.ds(pl.multiple_of(t * tile, 128), tile)
        gate = jnp.dot(x, weights[0, depth, lanes], preferred_element_type=f32)
        up = jnp.dot(x, weights[1, depth, lanes], preferred_element_type=f32)
        return gate, up

    loads[0].wait()
    loads[1].wait()

    def own_piece(t, _):
        gate, up = products(rep, t)
        hidden_sum[t, :, :tile] = gate
        hidden_sum[t, :, tile:] = up
        return 0

    lax.fori_loop(0, 4, own_piece, 0)
    for copy in pending:
        copy.wait()
    sums = []
    for i in range(2):
        t = 2 * (1 - rep) + i
        gate, up = products(1 - rep, t)
        sent_sum[i, :, :tile] = (hidden_sum[t, :, :tile] + gate).astype(bf16)
        sent_sum[i, :, tile:] = (hidden_sum[t, :, tile:] + up).astype(bf16)
        sums.append(send(sent_sum.at[i], other_sum.at[i], sum_sems, (i,), to_rep))

    def other_piece(i, _):
        t = 2 * rep + i
        gate, up = products(1 - rep, t)
        hidden_sum[t, :, :tile] += gate
        hidden_sum[t, :, tile:] += up
        return 0

    lax.fori_loop(0, 2, other_piece, 0)
    active = []
    for i in range(2):
        sums[i].wait()
        t = 2 * rep + i
        gate = hidden_sum[t, :, :tile] + other_sum[i, :, :tile].astype(f32)
        up = hidden_sum[t, :, tile:] + other_sum[i, :, tile:].astype(f32)
        activated[rep, i] = (gate / (1.0 + jnp.exp(-gate)) * up).astype(bf16)
        active.append(
            send(activated.at[rep, i], activated.at[rep, i], active_sems, (i,), to_rep)
        )

    def down(side, j):
        total = jnp.zeros((count, chunk), f32)
        for i in range(2):
            rows = pl.ds(pl.multiple_of(j * chunk, 128), chunk)
            lanes = pl.ds(pl.multiple_of((2 * side + i) * tile, 128), tile)
            total += lax.dot_general(
                activated[side, i],
                weights[2, rows, lanes],
                (((1,), (1,)), ((), ())),
                preferred_element_type=f32,
            )
        return total

    loads[2].wait()
    share_core.wait()
    every = shares[...].reshape(count, shares.shape[4])
    expert = lax.broadcasted_iota(jnp.int32, every.shape, 1)
    mix = jnp.sum(
        jnp.where(expert == 4 * far + 2 * near + core, every, 0.0), axis=1, keepdims=True
    )

    def own_hidden(j, _):
        out_sum[j] = down(rep, j)
        return 0

    lax.fori_loop(0, 4, own_hidden, 0)
    for copy in active:
        copy.wait()

    def finish(j):
        out = (out_sum[j] + down(1 - rep, j)) * mix
        out_ref[j] = out.astype(bf16).reshape(2 * n_far, 2, own, chunk)

    back = []
    for k in range(2):
        finish(2 * (1 - rep) + k)
        back.append(
            send(out_ref.at[2 * (1 - rep) + k], from_rep.at[k], back_sems, (k,), to_rep)
        )

    def finish_own(k, _):
        finish(2 * rep + k)
        return 0

    lax.fori_loop(0, 2, finish_own, 0)

    scatter = Scatter(
        spot, links, source2, from_core2, half2, from_near2, quarter2, from_far2, sems2
    )
    first = []
    for k in range(2):
        back[k].wait()

        def arrange(j, _):
            mine = out_ref[2 * rep + k, j // 2, j % 2]
            other = from_rep[k, j // 2, j % 2]
            source2[k, j // 2, j % 2, 0] = jnp.where(flag == 0, mine, other)
            source2[k, j // 2, j % 2, 1] = jnp.where(flag == 0, other, mine)
            return 0

        lax.fori_loop(0, 4 * n_far, arrange, 0)
        first.append(scatter.first(k))
        if k == 0:
            first[0].wait()
            second = [scatter.second(0)]
            second[0].wait()
            third = [scatter.third(0)]
    first[1].wait()
    second.append(scatter.second(1))
    second[1].wait()
    third.append(scatter.third(1))
    last = []
    for k in range(2):
        for copy in third[k]:
            copy.wait()
        layer = residual_ref[:, :, k * chunk : (k + 1) * chunk] + scatter.total(k)
        layer = layer.astype(bf16)
        for h in range(2):
            lanes = pl.ds(pl.multiple_of((2 * h + rep) * piece + k * chunk, 128), chunk)
            layer_ref[:, lanes] = layer[h]
            block = layer_ref.at[:, lanes]
            last.append(send(block, block, last_sems, (2 * k + h,), to_rep))
    for copy in last:
        copy.wait()


def layer(n_ep, flag, heads, projection, hidden, gain, share, weights):
    n_far = n_ep // 4
    own, width = hidden.shape
    piece = width // 4
    chunk = piece // 2
    count = n_ep * own
    units = weights.shape[2]
    tile = units // 4
    f32, bf16 = jnp.float32, jnp.bfloat16
    vmem = pl.BlockSpec(memory_space=pltpu.VMEM)
    return pl.pallas_call(
        functools.partial(layer_kernel, n_far),
        out_shape=jax.ShapeDtypeStruct((own, width), bf16),
        in_specs=[pl.BlockSpec(memory_space=pltpu.SMEM)]
        + [vmem] * 5
        + [pl.BlockSpec(memory_space=pl.ANY)],
        out_specs=vmem,
        scratch_shapes=scatter_scratch(n_far, 2, (own, piece))
        + scatter_scratch(n_far, 2, (2, own, chunk))
        + [
            pltpu.VMEM((2, 2, own, piece), bf16),
            pltpu.VMEM((2, own, piece), f32),
            pltpu.VMEM((n_far, 2, 2, 2, own, piece), bf16),
            pltpu.VMEM((n_far, 2, 2, own, piece), bf16),
            pltpu.VMEM((2, n_far, 2, 2, own, piece), bf16),
            pltpu.VMEM(weights.shape, bf16),
            pltpu.VMEM((4, count, 2 * tile), f32),
            pltpu.VMEM((2, count, 2 * tile), bf16),
            pltpu.VMEM((2, count, 2 * tile), bf16),
            pltpu.VMEM((2, 2, count, tile), bf16),
            pltpu.VMEM((4, count, chunk), f32),
            pltpu.VMEM((4, 2 * n_far, 2, own, chunk), bf16),
            pltpu.VMEM((2, 2 * n_far, 2, own, chunk), bf16),
            pltpu.SemaphoreType.DMA((3,)),
            pltpu.SemaphoreType.DMA((2, 2)),
            pltpu.SemaphoreType.DMA((2, 4 * n_far - 1)),
            pltpu.SemaphoreType.DMA((2, 4 * n_far)),
            pltpu.SemaphoreType.DMA((2, 2)),
            pltpu.SemaphoreType.DMA((2, 2)),
            pltpu.SemaphoreType.DMA((2, 2)),
            pltpu.SemaphoreType.DMA((2, 4)),
            pltpu.VMEM((n_far, 2, 2) + share.shape, f32),
            pltpu.SemaphoreType.DMA((2, n_far + 1)),
        ],
        compiler_params=pltpu.CompilerParams(
            collective_id=0, has_side_effects=True, vmem_limit_bytes=VMEM_BYTES
        ),
    )(flag, heads, projection, hidden, gain, share, weights)


def on_device(
    hidden_in,
    queries,
    new_keys,
    new_values,
    cache_keys,
    cache_values,
    cache_lengths,
    expert_ids,
    router_logits,
    norm_gain,
    out_sectioned,
    expert_sectioned,
    bucket_owner,
):
    steps, row_block, width = hidden_in.shape
    n_ep = lax.axis_size("ep")
    n_rep = lax.axis_size("rep")
    me_rep = lax.axis_index("rep")
    me_ep = lax.axis_index("ep")
    half = width // n_rep
    own = steps * row_block
    part = own // n_rep
    f32, bf16 = jnp.float32, jnp.bfloat16
    owners = bucket_owner[0]
    bucket_of = jnp.argsort(owners)

    affinity = jax.nn.sigmoid(router_logits)
    share = ROUTE_SCALE * affinity / jnp.sum(affinity, axis=2, keepdims=True)
    experts = jnp.arange(n_ep, dtype=jnp.int32)
    dense = jnp.sum(jnp.where(expert_ids[..., None] == experts, share[..., None], 0.0), axis=2)
    dense = dense.transpose(1, 0, 2).reshape(own, n_ep)

    heads = attention(queries, new_keys, new_values, cache_keys, cache_values, cache_lengths)
    heads = heads.reshape(n_ep * own, -1)
    hidden = hidden_in.transpose(1, 0, 2).reshape(own, width)
    weights = expert_sectioned[0]
    by_kernel = n_rep == 2 and n_ep % 4 == 0 and own % 16 == 0 and half % 512 == 0
    if by_kernel and weights.shape[2] % 512 == 0:
        flag = (owners[0] != me_rep).astype(jnp.int32).reshape(1, 1)
        out = layer(
            n_ep,
            flag,
            heads,
            out_sectioned,
            hidden,
            norm_gain[None],
            jnp.pad(dense, ((0, 0), (0, -n_ep % 128))),
            weights.transpose(1, 0, 2),
        )
        return out.reshape(row_block, steps, width).transpose(1, 0, 2)
    partial = jnp.dot(heads, out_sectioned, preferred_element_type=f32).astype(bf16)
    summed = lax.psum_scatter(partial, "ep", scatter_dimension=0, tiled=True)
    swapped = lax.all_to_all(
        summed.reshape(n_rep, part, half), "rep", split_axis=0, concat_axis=0, tiled=True
    )
    attended = swapped.transpose(1, 0, 2).reshape(part, width)
    hidden = lax.dynamic_slice_in_dim(hidden, me_rep * part, part, 0)
    residual = hidden.astype(f32) + attended.astype(f32)
    mean_square = jnp.mean(residual * residual, axis=1, keepdims=True)
    normalized = (residual * lax.rsqrt(mean_square + EPSILON) * norm_gain).astype(bf16)

    gathered = lax.all_gather(normalized, "ep", axis=0, tiled=True)
    blocks = gathered.reshape(n_ep * part, n_rep, half).transpose(1, 0, 2)
    blocks = jnp.take(blocks, bucket_of, axis=0)
    arrived = lax.all_to_all(blocks, "rep", split_axis=0, concat_axis=0, tiled=True)
    arrived = arrived.reshape(n_rep * n_ep * part, half)

    mix = lax.all_gather(dense, "ep", axis=0, tiled=False)
    mix = lax.dynamic_index_in_dim(mix, me_ep, axis=2, keepdims=False)
    mix = mix.reshape(n_ep, n_rep, part).transpose(1, 0, 2)
    mix = mix.reshape(-1, 1)
    gate = jnp.dot(arrived, weights[:, 0], preferred_element_type=f32).astype(bf16)
    up = jnp.dot(arrived, weights[:, 1], preferred_element_type=f32).astype(bf16)
    both = jnp.stack([gate, up])
    both = lax.psum_scatter(both, "rep", scatter_dimension=1, tiled=True).astype(f32)
    activated = (jax.nn.silu(both[0]) * both[1]).astype(bf16)
    activated = lax.all_gather(activated, "rep", axis=0, tiled=True)
    out = jnp.einsum("nf,df->nd", activated, weights[:, 2], preferred_element_type=f32)
    out = (out * mix).astype(bf16)

    back = lax.all_to_all(
        out.reshape(n_rep, n_ep * part, half), "rep", split_axis=0, concat_axis=0, tiled=True
    )
    back = jnp.take(back, owners, axis=0).transpose(1, 0, 2).reshape(n_ep * part, width)
    routed = lax.psum_scatter(back, "ep", scatter_dimension=0, tiled=True)
    result = (residual + routed.astype(f32)).astype(bf16)
    result = lax.all_gather(result, "rep", axis=0, tiled=True)
    return result.reshape(row_block, steps, width).transpose(1, 0, 2)


def solution(mesh):
    return jax.shard_map(
        on_device,
        mesh=mesh,
        in_specs=(
            P(None, "ep", None),
            P(None, None, "ep"),
            P(None, None, "ep"),
            P(None, None, "ep"),
            P(None, None, "ep"),
            P(None, None, "ep"),
            P(),
            P(None, "ep", None),
            P(None, "ep", None),
            P(),
            P("ep", "rep"),
            P("ep", "rep", None, None),
            P("ep", None),
        ),
        out_specs=P(None, "ep", None),
        check_vma=False,
    )
```
